32 devices in a mesh: groups: 2 (over y), tensor: 4 (over z), dp: 4 (over x, core).
Axes of the slice: x: 2, y: 2, z: 4, core: 2. Of those that a mesh axis runs over, the one named last changes fastest.
Arguments:
- tokens: bfloat16 [8192, 6144], P(('groups', 'dp'), 'tensor'), parts along dimension 0, may hold values from -6 to 6
- cotangent: bfloat16 [8192, 6144], P(('groups', 'dp'), 'tensor'), parts along dimension 0, may hold values from -6 to 6
- right_in: bfloat16 [64, 96, 384], P('tensor'), may hold values from -0.625 to 0.625
- left_in: bfloat16 [64, 384, 384], P('tensor'), may hold values from -0.3125 to 0.3125
- right_out: bfloat16 [64, 384, 384], P('tensor'), may hold values from -0.3125 to 0.3125
- left_out: bfloat16 [64, 384, 96], P('tensor'), may hold values from -0.3125 to 0.3125
Outputs:
- output: bfloat16 [8192, 6144], P(('groups', 'dp'), 'tensor'), parts along dimension 0
- grad_tokens: bfloat16 [8192, 6144], P(('groups', 'dp'), 'tensor'), parts along dimension 0
- grad_right_in: float32 [128, 96, 384], P(('groups', 'tensor'), None, 'dp'), parts along dimension 0
- grad_left_in: float32 [128, 384, 384], P(('groups', 'tensor'), None, 'dp'), parts along dimension 0
- grad_right_out: float32 [128, 384, 384], P(('groups', 'tensor'), None, 'dp'), parts along dimension 0
- grad_left_out: float32 [128, 384, 96], P(('groups', 'tensor'), 'dp'), parts along dimension 0
The draws below stay inside these ranges and needn't reach their ends.
There are 2 independent parts, one for each index of `groups`. The reference program is written for one: setup_inputs(seed, part) draws one part's arguments, and reference() takes and returns one part's arrays. A program takes and returns all parts, laid end to end along the dimension named above; an argument that names none is the same for every part. Nothing has to cross between parts.
All inputs are finite; a program needn't handle non-finite values.
Results may differ from the reference program's by a relative error of at most 0.0068.
Values may be sent and summed in bfloat16 or wider, within the bound.
No kernel may reach another device: no remote copies, remote signals or barrier semaphores. Data moves between devices by JAX's collectives and lax.ppermute only.
A program may use at most 320 MiB of HBM per device.

```python
import math
import jax
import jax.numpy as jnp
from jax import lax

D = 6144
NB = 64
TOKENS = 4096
BI = 96
BH = 384
SUB = 6


def levels(own_key, dims, cuts, least, largest):
    gain, own = 1.0, jax.random.fold_in(own_key, 6)
    for position, blocks in cuts:
        draws = jnp.exp(jax.random.uniform(jax.random.fold_in(own, position), (blocks,), jnp.float32, least / len(cuts), largest / len(cuts)))
        gain = gain * jnp.repeat(draws, dims[position] // blocks).reshape([-1 if axis == position else 1 for axis in range(len(dims))])
    return gain


def normal_values(rng, dims, spread, reach, split=(), dtype=jnp.bfloat16):
    loudness = levels(rng, dims, split, -0.22, 0.18) if split else 1.0
    array = jax.random.normal(rng, dims, jnp.float32) * spread * loudness
    return jnp.minimum(jnp.maximum(array, -reach), reach).astype(dtype)


def setup_inputs(seed: int = 0, part: int = 0) -> dict:
    key_of = jax.random.split(jax.random.key(seed), 7)
    own_keys = jax.random.split(jax.random.fold_in(key_of[6], part), 7)
    tokens = normal_values(own_keys[0], (TOKENS, D), 1.0, 6.0, ((0, 4), (1, 4)))
    cotangent = normal_values(own_keys[1], (TOKENS, D), 1.0, 6.0, ((0, 4), (1, 4)))
    right_in = normal_values(key_of[2], (NB, BI, BH), BI ** -0.5, 0.625, ((0, 4),))
    left_in = normal_values(key_of[3], (NB, BH, BH), BH ** -0.5, 0.3125, ((0, 4),))
    right_out = normal_values(key_of[4], (NB, BH, BH), BH ** -0.5, 0.3125, ((0, 4),))
    left_out = normal_values(key_of[5], (NB, BH, BI), BH ** -0.5, 0.3125, ((0, 4),))
    return dict(tokens=tokens, cotangent=cotangent, right_in=right_in, left_in=left_in, right_out=right_out, left_out=left_out)


def gelu_back(pre, upstream):
    return jax.vjp(jax.nn.gelu, pre)[1](upstream)[0]

def permute_blocks(values):
    count = values.shape[0]
    return values.reshape(count, NB, NB, SUB).transpose(0, 2, 1, 3).reshape(count, NB, BH)

def reference(tokens, cotangent, right_in, left_in, right_out, left_out):
    f32 = jnp.float32
    ri = right_in.astype(f32)
    li = left_in.astype(f32)
    ro = right_out.astype(f32)
    lo = left_out.astype(f32)
    block_rows = math.gcd(TOKENS, 1024)
    steps_count = TOKENS // block_rows
    xs = tokens.reshape(steps_count, block_rows, NB, BI)
    gs = cotangent.reshape(steps_count, block_rows, NB, BI)

    def step(carry, pieces):
        g_ri, g_li, g_ro, g_lo = carry
        xb, gb = pieces
        blocks = xb.astype(f32)
        back = gb.astype(f32)
        first = jnp.einsum('tbi,bij->tbj', blocks, ri).astype(jnp.bfloat16)
        mixed_in = permute_blocks(first).astype(f32)
        pre = jnp.einsum('tck,ckm->tcm', mixed_in, li)
        hidden = jax.nn.gelu(pre).astype(jnp.bfloat16).astype(f32)
        second = jnp.einsum('tcm,cmn->tcn', hidden, ro).astype(jnp.bfloat16)
        mixed_out = permute_blocks(second).astype(f32)
        out = jnp.einsum('tdk,dkn->tdn', mixed_out, lo).astype(jnp.bfloat16)
        back_mixed = jnp.einsum('tdn,dkn->tdk', back, lo).astype(jnp.bfloat16)
        back_second = permute_blocks(back_mixed).astype(f32)
        back_hidden = jnp.einsum('tcn,cmn->tcm', back_second, ro)
        back_pre = gelu_back(pre, back_hidden).astype(jnp.bfloat16).astype(f32)
        back_mixed_in = jnp.einsum('tcm,ckm->tck', back_pre, li).astype(jnp.bfloat16)
        back_first = permute_blocks(back_mixed_in).astype(f32)
        grad_x = jnp.einsum('tbj,bij->tbi', back_first, ri).astype(jnp.bfloat16)
        g_ri = g_ri + jnp.einsum('tbi,tbj->bij', blocks, back_first)
        g_li = g_li + jnp.einsum('tck,tcm->ckm', mixed_in, back_pre)
        g_ro = g_ro + jnp.einsum('tcm,tcn->cmn', hidden, back_second)
        g_lo = g_lo + jnp.einsum('tdk,tdn->dkn', mixed_out, back)
        return ((g_ri, g_li, g_ro, g_lo), (out, grad_x))
    init = (jnp.zeros((NB, BI, BH), f32), jnp.zeros((NB, BH, BH), f32), jnp.zeros((NB, BH, BH), f32), jnp.zeros((NB, BH, BI), f32))
    grads, outs = lax.scan(step, init, (xs, gs))
    scale = 1.0 / math.sqrt(TOKENS)
    output = outs[0].reshape(TOKENS, D)
    grad_tokens = outs[1].reshape(TOKENS, D)
    return (output, grad_tokens, grads[0] * scale, grads[1] * scale, grads[2] * scale, grads[3] * scale)
```

```python
import functools
import math

import jax
import jax.numpy as jnp
from jax import lax
from jax.experimental import pallas as pl
from jax.experimental.pallas import tpu as pltpu
from jax.sharding import Mesh
from jax.sharding import PartitionSpec as P

F32 = jnp.float32
BF16 = jnp.bfloat16
PACK = 8
TAIL = 4
LANES = 128
VMEM = 56 * 1024 * 1024


def dot(a, b, contract):
    return lax.dot_general(a, b, ((contract[:1], contract[1:]), ((), ())), preferred_element_type=F32)


def scratch(blocks, rows, lanes):
    return pltpu.VMEM((lanes // LANES, blocks * (rows + 1), LANES), F32)


def spread_kernel(steps, blocks, part, pos_ref, *refs):
    *act_refs, w_ref, out_ref, buf = refs
    step = pl.program_id(0)
    wide, rows = w_ref.shape[2:]
    tiles = act_refs[0].shape[1] // LANES
    pitch = rows + 1

    @pl.when(step < steps)
    def _():
        at = pl.ds(pl.multiple_of(step * PACK * pitch, 8), PACK * pitch)
        for p in range(PACK):
            for n, ref in enumerate(act_refs):
                first = dot(w_ref[p, 0], ref[0, :, p * wide : (p + 1) * wide], (0, 1))
                for k in range(tiles):
                    buf.at[n * tiles + k, at, :][p * pitch : p * pitch + rows, :] = first[:, k * LANES : (k + 1) * LANES]

    @pl.when(step >= steps)
    def _():
        for p in range(TAIL):
            c = (step - steps) * TAIL + p
            for s in range(part):
                for k in range(buf.shape[0]):
                    rest = buf[k, pl.ds(c * part + s, blocks, stride=pitch), :]
                    out_ref[p, s * blocks : (s + 1) * blocks, k * LANES : (k + 1) * LANES] = rest.astype(BF16)


def spread(pos, acts, w, which, part):
    blocks, _, wide, rows = w.shape
    quarters, count, span = acts[0].shape
    lanes = count * len(acts)
    steps = blocks // PACK
    per = span // (PACK * wide)
    own_c = rows // part

    def act_map(i, pos):
        j = jnp.minimum(i, steps - 1)
        return j // per, 0, lax.rem(j, per)

    def w_map(i, pos):
        j = jnp.minimum(i, steps - 1)
        return lax.rem(j // per + 4 - pos[0], 4) * per + lax.rem(j, per), which, 0, 0

    return pl.pallas_call(
        functools.partial(spread_kernel, steps, blocks, part),
        grid_spec=pltpu.PrefetchScalarGridSpec(
            num_scalar_prefetch=1,
            grid=(steps + own_c // TAIL,),
            in_specs=[pl.BlockSpec((1, count, PACK * wide), act_map)] * len(acts) + [pl.BlockSpec((PACK, 1, wide, rows), w_map)],
            out_specs=pl.BlockSpec((TAIL, blocks * part, lanes), lambda i, pos: (jnp.maximum(i - steps, 0), 0, 0)),
            scratch_shapes=[scratch(blocks, rows, lanes)],
        ),
        out_shape=jax.ShapeDtypeStruct((own_c, blocks * part, lanes), BF16),
        compiler_params=pltpu.CompilerParams(vmem_limit_bytes=VMEM),
        cost_estimate=pl.CostEstimate(flops=2 * blocks * rows * wide * lanes, bytes_accessed=58_000_000, transcendentals=0),
        name="spread",
    )(pos, *acts, w)


def gather_kernel(lead, blocks, part, pos_ref, mixed_ref, *refs):
    *act_refs, w_ref, keep_ref, send_ref, grad_ref, buf = refs
    step = pl.program_id(0)
    wide, rows = w_ref.shape[2:]
    count = act_refs[0].shape[1]
    pitch = rows + 1

    @pl.when(step < lead)
    def _():
        for p in range(TAIL):
            c = step * TAIL + p
            for s in range(part):
                for k in range(buf.shape[0]):
                    rest = mixed_ref[p, s * blocks : (s + 1) * blocks, k * LANES : (k + 1) * LANES]
                    buf[k, pl.ds(c * part + s, blocks, stride=pitch), :] = rest.astype(F32)

    @pl.when(step >= lead)
    def _():
        quarter_steps = (blocks // PACK) // 4
        r = (step - lead) // quarter_steps
        t = lax.rem(r + pos_ref[0], 4)
        group = t * quarter_steps + lax.rem(step - lead, quarter_steps)
        at = pl.ds(pl.multiple_of(group * PACK * pitch, 8), PACK * pitch)
        outs = []
        for p in range(PACK):
            tiles = [buf.at[k, at, :][p * pitch : p * pitch + rows, :].astype(BF16) for k in range(buf.shape[0])]
            z = jnp.concatenate(tiles, axis=1)
            outs.append(dot(w_ref[p, 0], z, (1, 0)))
            g = 0.0
            for n, ref in enumerate(act_refs):
                g = g + dot(z[:, n * count : (n + 1) * count], ref[0, :, p * wide : (p + 1) * wide], (1, 0))
            top, left = divmod(p, PACK // 2)
            grad_ref[0, top, :, left * wide : (left + 1) * wide] = g.astype(BF16)
        out = jnp.concatenate(outs, axis=0).T.astype(BF16)
        for n in range(len(act_refs)):
            ref = keep_ref if n < len(act_refs) // 2 else send_ref
            ref[n % (len(act_refs) // 2), 0] = out[n * count : (n + 1) * count]


def gather(pos, mixed, acts, w, which, part):
    blocks, _, wide, rows = w.shape
    quarters, count, span = acts[0].shape
    half = len(acts) // 2
    lanes = count * len(acts)
    per = span // (PACK * wide)
    own_c = rows // part
    lead = own_c // TAIL
    steps = blocks // PACK

    def place(i, pos):
        j = jnp.maximum(i - lead, 0)
        return lax.rem(j // per + pos[0], 4), lax.rem(j, per)

    def act_map(i, pos):
        t, k = place(i, pos)
        return t, 0, k

    def out_map(i, pos):
        t, k = place(i, pos)
        return 0, t, 0, k

    act = pl.BlockSpec((1, count, PACK * wide), act_map)
    out = pl.BlockSpec((half, 1, count, PACK * wide), out_map)
    return pl.pallas_call(
        functools.partial(gather_kernel, lead, blocks, part),
        grid_spec=pltpu.PrefetchScalarGridSpec(
            num_scalar_prefetch=1,
            grid=(lead + steps,),
            in_specs=[pl.BlockSpec((TAIL, blocks * part, lanes), lambda i, pos: (jnp.minimum(i, lead - 1), 0, 0))]
            + [act] * len(acts)
            + [pl.BlockSpec((PACK, 1, wide, rows), lambda i, pos: (jnp.maximum(i - lead, 0), which, 0, 0))],
            out_specs=[out, out, pl.BlockSpec((1, 2, rows, PACK // 2 * wide), lambda i, pos: (jnp.maximum(i - lead, 0), 0, 0, 0))],
            scratch_shapes=[scratch(blocks, rows, lanes)],
        ),
        out_shape=[jax.ShapeDtypeStruct((half, quarters, count, span), BF16)] * 2
        + [jax.ShapeDtypeStruct((steps, 2, rows, PACK // 2 * wide), BF16)],
        compiler_params=pltpu.CompilerParams(vmem_limit_bytes=VMEM),
        cost_estimate=pl.CostEstimate(flops=4 * blocks * rows * wide * lanes, bytes_accessed=76_000_000, transcendentals=0),
        name="gather",
    )(pos, mixed, *acts, w)


K0 = math.sqrt(2.0 / math.pi)


def forward_kernel(at_ref, wat_ref, m_ref, li_ref, ro_ref, *refs):
    out_ref = refs[-1]
    pre = dot(li_ref[0, 0], m_ref[0], (0, 0))
    hidden = pre * (0.5 * (1.0 + jnp.tanh(K0 * (pre + 0.044715 * (pre * pre * pre)))))
    out_ref[0] = dot(ro_ref[0, 0], hidden.astype(BF16), (0, 0)).astype(BF16)


def forward(at, wat, mixed, w, second):
    count = at.shape[0]
    _, hid, tokens = mixed.shape
    act = pl.BlockSpec((1, hid, tokens), lambda i, at, wat: (at[i], 0, 0))
    old = [] if second is None else [second]
    return pl.pallas_call(
        forward_kernel,
        grid_spec=pltpu.PrefetchScalarGridSpec(
            num_scalar_prefetch=2,
            grid=(count,),
            in_specs=[
                act,
                pl.BlockSpec((1, 1, hid, hid), lambda i, at, wat: (wat[i], 0, 0, 0)),
                pl.BlockSpec((1, 1, hid, hid), lambda i, at, wat: (wat[i], 1, 0, 0)),
            ]
            + [pl.BlockSpec(memory_space=pl.ANY)] * len(old),
            out_specs=act,
        ),
        out_shape=jax.ShapeDtypeStruct(mixed.shape, BF16),
        input_output_aliases={5: 0} if old else {},
        compiler_params=pltpu.CompilerParams(vmem_limit_bytes=VMEM),
        cost_estimate=pl.CostEstimate(flops=4 * count * hid * hid * tokens, bytes_accessed=count * 8_000_000, transcendentals=0),
        name="forward",
    )(at, wat, mixed, w, w, *old)


def backward_kernel(blocks, at_ref, wat_ref, m_ref, b_ref, li_ref, ro_ref, b_out, grad_ref, bp):
    m = m_ref[0]
    li = li_ref[0, 0]
    pre = dot(li, m, (0, 0))
    square = pre * pre
    th = jnp.tanh(K0 * (pre * (1.0 + 0.044715 * square)))
    cdf = 0.5 * (1.0 + th)
    hidden = (pre * cdf).astype(BF16)
    slope = cdf + pre * (0.5 * K0) * (1.0 - th * th) * (1.0 + (3.0 * 0.044715) * square)
    bp[...] = (dot(ro_ref[0, 0], b_ref[0], (1, 0)) * slope).astype(BF16)
    b_out[0] = dot(li, bp[...], (1, 0)).astype(BF16)
    g_li = dot(bp[...], m, (1, 1)).astype(BF16)
    g_ro = dot(b_ref[0], hidden, (1, 1)).astype(BF16)
    chunks, rows = grad_ref.shape[2:4]
    piece = blocks // chunks
    for q in range(chunks):
        grad_ref[0, 0, q] = g_li[q * rows : (q + 1) * rows]
        for s in range(rows // piece):
            start = s * blocks + q * piece
            grad_ref[0, 1, q, s * piece : (s + 1) * piece, :] = g_ro[start : start + piece]


def backward(at, wat, mixed, back, w, blocks):
    count = at.shape[0]
    _, hid, tokens = mixed.shape
    act = pl.BlockSpec((1, hid, tokens), lambda i, at, wat: (at[i], 0, 0))
    return pl.pallas_call(
        functools.partial(backward_kernel, blocks),
        grid_spec=pltpu.PrefetchScalarGridSpec(
            num_scalar_prefetch=2,
            grid=(count,),
            in_specs=[
                act,
                act,
                pl.BlockSpec((1, 1, hid, hid), lambda i, at, wat: (wat[i], 0, 0, 0)),
                pl.BlockSpec((1, 1, hid, hid), lambda i, at, wat: (wat[i], 1, 0, 0)),
            ],
            out_specs=[act, pl.BlockSpec((1, 2, 4, hid // 4, hid), lambda i, at, wat: (i, 0, 0, 0, 0))],
            scratch_shapes=[pltpu.VMEM((hid, tokens), BF16)],
        ),
        out_shape=[jax.ShapeDtypeStruct(mixed.shape, BF16), jax.ShapeDtypeStruct((count, 2, 4, hid // 4, hid), BF16)],
        input_output_aliases={3: 0},
        compiler_params=pltpu.CompilerParams(vmem_limit_bytes=VMEM),
        cost_estimate=pl.CostEstimate(flops=10 * count * hid * hid * tokens, bytes_accessed=count * 15_000_000, transcendentals=0),
        name="backward",
    )(at, wat, mixed, back, w, w)


def swap(a, axis):
    return lax.ppermute(a, axis, [(0, 1), (1, 0)])


def after(value, *others):
    return lax.optimization_barrier((value, *others))[0]


def up(a, first, last):
    return lax.ppermute(a, "tensor", [(i, i + 1) for i in range(first, last)])


def down(a, first, last):
    return lax.ppermute(a, "tensor", [(i, i - 1) for i in range(first, last, -1)])


def add(*terms):
    total = terms[0].astype(F32)
    for term in terms[1:]:
        total = total + term.astype(F32)
    return total


def all_to_all(a):
    return lax.all_to_all(a, "tensor", split_axis=0, concat_axis=0, tiled=True)


def tokens_plan(tokens, cotangent, right_in, left_in, right_out, left_out):
    g = lax.axis_index("groups")
    z = lax.axis_index("tensor")
    x = lax.axis_index("x")
    core = lax.axis_index("core")
    mate = 2 * x + core
    rows, span = tokens.shape
    nb, wide, hid = right_in.shape
    blocks = 4 * nb
    part = hid // blocks
    own_nb = nb // 4
    scale = 1.0 / math.sqrt(rows * 4)
    pos = jnp.stack([z, x]).astype(jnp.int32)

    place = jnp.arange(hid)
    reorder = (place[:, None] % blocks * part + place[:, None] // blocks == place[None, :]).astype(BF16)

    def line_gather(a):
        u1, d1 = up(a, 0, 3), down(a, 3, 0)
        u2, d2 = up(u1, 1, 3), down(d1, 2, 0)
        u3, d3 = up(u2, 2, 3), down(d2, 1, 0)
        return jnp.stack([jnp.where(z == 3, u3, d1), jnp.where(z < 2, d2, u2), jnp.where(z == 0, d3, u1)])

    def by_group(a, b):
        return jnp.where(g == 0, jnp.stack([a, b], axis=1), jnp.stack([b, a], axis=1))

    small = jnp.stack([right_in, jnp.swapaxes(left_out, 1, 2)], axis=1)
    small = small.reshape(nb, 2, wide, 4, 4, own_nb * part)
    small = lax.dynamic_index_in_dim(small, mate, axis=4, keepdims=False).reshape(nb, 2, wide, hid // 4)
    fs = line_gather(lax.dynamic_slice_in_dim(small, g * (nb // 2), nb // 2, axis=0))

    own_li = lax.dynamic_slice_in_dim(left_in, mate * own_nb, own_nb, axis=0)
    own_ro = lax.dynamic_slice_in_dim(right_out, mate * own_nb, own_nb, axis=0)
    own_li = jnp.einsum("pk,ckm->cpm", reorder, own_li, preferred_element_type=F32).astype(BF16)
    own_ro = jnp.einsum("cmn,pn->cmp", own_ro, reorder, preferred_element_type=F32).astype(BF16)
    own_w = jnp.stack([own_li, own_ro], axis=1)

    own_x = all_to_all(tokens.reshape(4, rows // 4, span))
    x_x = swap(own_x, "x")
    cotangent, mine, own_x, fs = lax.optimization_barrier((cotangent, lax.dynamic_slice_in_dim(own_w, 2 * g, 2, axis=0), own_x, fs))
    own_y = all_to_all(cotangent.reshape(4, rows // 4, span))
    acts_x = [own_x, x_x, swap(own_x, "core"), swap(x_x, "core")]
    f = line_gather(mine)
    yf = swap(f, "groups")
    x_y = swap(own_y, "x")
    small = jnp.concatenate([small, by_group(fs, swap(fs, "groups")).reshape(3 * nb, *small.shape[1:])])

    order = [(gr, h) for gr in range(2) for h in range(2)]
    index = {(gr, h): 2 * ((g + gr) % 2) + h for gr, h in order}
    six = jnp.arange(6, dtype=jnp.int32)
    pieces = [
        (jnp.stack([z * own_nb + index[o] for o in order]).astype(jnp.int32), jnp.stack([index[o] for o in order]).astype(jnp.int32), own_w)
    ]
    for gr, w in enumerate((f, yf)):
        at = [(z + r) % 4 * own_nb + index[gr, h] for r in (1, 2, 3) for h in range(2)]
        pieces.append((jnp.stack(at).astype(jnp.int32), six, w.reshape(6, 2, hid, hid)))

    mixed = spread(pos, acts_x, small, 0, part)
    second = None
    for at, wat, w in pieces:
        if w is pieces[2][2]:
            second, x_y = lax.optimization_barrier((second, x_y))
        second = forward(at, wat, mixed, w, second)
    acts_y = [own_y, x_y, swap(own_y, "core"), swap(x_y, "core")]
    keep, send, lo = gather(pos, second, acts_y, small, 1, part)
    got = swap(send, "core")
    back = spread(pos, acts_y, small, 1, part)
    back, got = lax.optimization_barrier((back, got))
    out_x = swap(add(keep[1], got[1]).astype(BF16), "x")
    out = add(keep[0], got[0])

    grads = {}

    def step(n):
        at, wat, w = pieces[n]
        return backward(at, wat, mixed, back, w, blocks)

    def shares(n, first):
        first = first.reshape(4, -1, hid // 4, hid)
        by_place = grads[n].reshape(3, -1, hid // 4, hid)
        return [jnp.concatenate([by_place[r], first[r + 1]]) for r in range(3)]

    def first_hop(s):
        return up(s[2], 0, 1), down(s[0], 3, 2)

    def second_hop(s, u, d):
        return up(add(s[1], u).astype(BF16), 0, 2), down(add(s[1], d).astype(BF16), 3, 1)

    def third_hop(s, u, d):
        return up(add(s[0], u).astype(BF16), 0, 3), down(add(s[2], d).astype(BF16), 3, 0)

    back, grads[1] = step(1)
    s1 = shares(1, lo)
    u, d = first_hop(s1)
    back, grads[2] = step(2)
    back, u, d = lax.optimization_barrier((back, u, d))
    u, d = second_hop(s1, u, d)
    back, grads[0] = step(0)
    back, out_x, u, d = lax.optimization_barrier((back, out_x, u, d))
    output = all_to_all(add(out, out_x).astype(BF16)).reshape(rows, span)
    u1, d1 = third_hop(s1, u, d)
    keep, send, ri = gather(pos, back, acts_x, small, 0, part)
    got = swap(send, "core")
    gx_x = swap(add(keep[1], got[1]).astype(BF16), "x")
    s2 = shares(2, ri)
    u, d = first_hop(s2)
    u, d = second_hop(s2, u, d)
    u, d, gx_x = lax.optimization_barrier((u, d, gx_x))
    grad_tokens = all_to_all(add(add(keep[0], got[0]), gx_x).astype(BF16)).reshape(rows, span)
    v1, e1 = third_hop(s2, u, d)

    def reduced(n, first, u1, d1):
        own = grads[0].reshape(2, -1, hid // 4, hid)[n - 1]
        count = own.shape[0]
        total = add(jnp.concatenate([own, first.reshape(4, -1, hid // 4, hid)[0]]), u1, d1).astype(BF16)
        second = total[:count].reshape(-1, 2, 2, hid // 4, hid).transpose(1, 2, 0, 3, 4).reshape(2, 2, -1, hid)
        first = total[count:].reshape(-1, 2, 2, hid // 16, hid).transpose(1, 2, 0, 3, 4).reshape(2, 2, -1, hid)
        total = jnp.concatenate([second, first], axis=2)
        kept = lax.dynamic_index_in_dim(total, x, axis=0, keepdims=False)
        got = swap(lax.dynamic_index_in_dim(total, 1 - x, axis=0, keepdims=False), "x")
        total = jnp.where(x == 0, jnp.stack([kept, got], axis=1), jnp.stack([got, kept], axis=1))
        kept = lax.dynamic_index_in_dim(total, core, axis=0, keepdims=False)
        got = swap(lax.dynamic_index_in_dim(total, 1 - core, axis=0, keepdims=False), "core")
        total = jnp.where(core == 0, jnp.stack([kept, got], axis=1), jnp.stack([got, kept], axis=1)).reshape(4, -1, hid)
        cut = second.shape[2]
        return total[:, :cut].reshape(4, 2, 2, hid // 4, hid), total[:, cut:].reshape(4, nb // PACK, 2, hid // 16, PACK // 2, wide)

    big0, grad_lo = reduced(1, lo, u1, d1)
    big1, grad_ri = reduced(2, ri, v1, e1)
    big = by_group(big0, big1).reshape(nb, 2, hid // 4, hid)
    grad_li = jnp.einsum("cmp,pk->cmk", big[:, 0], reorder, preferred_element_type=F32) * scale
    grad_li = jnp.swapaxes(grad_li, 1, 2)
    grad_ro = big[:, 1].reshape(nb, part, blocks // 4, hid).swapaxes(1, 2).reshape(nb, hid // 4, hid).astype(F32) * scale
    grad_ro = jnp.swapaxes(grad_ro, 1, 2)
    grad_lo = grad_lo.astype(F32).transpose(1, 2, 4, 0, 3, 5).reshape(nb, hid // 4, wide) * scale
    grad_ri = grad_ri.astype(F32).transpose(1, 2, 4, 5, 0, 3).reshape(nb, wide, hid // 4) * scale
    return (output, grad_tokens, grad_ri, grad_li, grad_ro, grad_lo)


def gelu_back(pre, upstream):
    return jax.vjp(jax.nn.gelu, pre)[1](upstream)[0]


def blocks_plan(tokens, cotangent, right_in, left_in, right_out, left_out):
    f32 = jnp.float32
    bf16 = jnp.bfloat16
    rows = tokens.shape[0]
    local_blocks = right_in.shape[0]
    block_in = right_in.shape[1]
    block_hid = right_in.shape[2]
    all_blocks = local_blocks * lax.axis_size("tensor")
    part_hid = block_hid // all_blocks
    scale = 1.0 / math.sqrt(rows * lax.axis_size("dp"))
    blocks = tokens.reshape(rows, local_blocks, block_in)
    back = cotangent.reshape(rows, local_blocks, block_in)
    ri_split = right_in.reshape(local_blocks, block_in, all_blocks, part_hid)
    first = jnp.einsum("tbi,bics->cbst", blocks, ri_split, preferred_element_type=f32)
    first = first.astype(bf16).reshape(all_blocks, local_blocks * part_hid, rows)
    ro_split = right_out.reshape(local_blocks, block_hid, all_blocks, part_hid)
    arrived_first = lax.all_to_all(first, "tensor", split_axis=0, concat_axis=1, tiled=True)
    count = arrived_first.shape[2]
    pre_act = jnp.einsum("ckt,ckm->cmt", arrived_first, left_in, preferred_element_type=f32)
    hidden_act = jax.nn.gelu(pre_act).astype(bf16)
    second_act = jnp.einsum("cmt,cmds->dcst", hidden_act, ro_split, preferred_element_type=f32)
    second_act = second_act.astype(bf16).reshape(all_blocks, local_blocks * part_hid, count)
    mixed_out = lax.all_to_all(second_act, "tensor", split_axis=0, concat_axis=1, tiled=True)
    output = jnp.einsum("dkt,dkn->tdn", mixed_out, left_out, preferred_element_type=f32)
    output = output.astype(bf16).reshape(rows, local_blocks * block_in)
    grad_lo = jnp.einsum("dkt,tdn->dkn", mixed_out, back, preferred_element_type=f32) * scale
    lo_split = left_out.reshape(local_blocks, all_blocks, part_hid, block_in)
    back_mixed = jnp.einsum("tdn,dcsn->cdst", back, lo_split, preferred_element_type=f32)
    back_mixed = back_mixed.astype(bf16).reshape(all_blocks, local_blocks * part_hid, rows)
    back_second = lax.all_to_all(back_mixed, "tensor", split_axis=0, concat_axis=1, tiled=True)
    grad_ro = (
        jnp.einsum("cmt,cnt->cmn", hidden_act, back_second, preferred_element_type=f32) * scale
    )
    back_hidden = jnp.einsum("cnt,cmn->cmt", back_second, right_out, preferred_element_type=f32)
    back_pre = gelu_back(pre_act, back_hidden).astype(bf16)
    grad_li = (
        jnp.einsum("ckt,cmt->ckm", arrived_first, back_pre, preferred_element_type=f32) * scale
    )
    li_split = left_in.reshape(local_blocks, all_blocks, part_hid, block_hid)
    back_in = jnp.einsum("cmt,cbsm->bcst", back_pre, li_split, preferred_element_type=f32)
    back_in = back_in.astype(bf16).reshape(all_blocks, local_blocks * part_hid, rows)
    back_first = lax.all_to_all(back_in, "tensor", split_axis=0, concat_axis=1, tiled=True)
    grad_x = jnp.einsum("bjt,bij->tbi", back_first, right_in, preferred_element_type=f32)
    grad_tokens = grad_x.astype(bf16).reshape(rows, local_blocks * block_in)
    grad_ri = jnp.einsum("tbi,bjt->bij", blocks, back_first, preferred_element_type=f32) * scale
    grad_ri, grad_li, grad_ro, grad_lo = (
        lax.psum_scatter(grad_ri, "dp", scatter_dimension=2, tiled=True),
        lax.psum_scatter(grad_li, "dp", scatter_dimension=2, tiled=True),
        lax.psum_scatter(grad_ro, "dp", scatter_dimension=2, tiled=True),
        lax.psum_scatter(grad_lo, "dp", scatter_dimension=1, tiled=True),
    )
    return (output, grad_tokens, grad_ri, grad_li, grad_ro, grad_lo)


def solution(mesh):
    wide = mesh.shape["tensor"] == 4 and mesh.shape["dp"] == 4 and mesh.shape["groups"] == 2
    dp = "dp"
    if wide:
        dp = ("x", "core")
        mesh = Mesh(mesh.devices.reshape(2, 4, 2, 2), ("groups", "tensor", *dp))
    row = ("groups", "x", "core") if wide else ("groups", "dp")
    acts = P(row, "tensor")
    placed = (acts, acts, P("tensor", None, None), P("tensor", None, None), P("tensor", None, None), P("tensor", None, None))
    own = ("groups", "tensor")
    return jax.shard_map(
        tokens_plan if wide else blocks_plan,
        mesh=mesh,
        in_specs=placed,
        out_specs=(acts, acts, P(own, None, dp), P(own, None, dp), P(own, None, dp), P(own, dp, None)),
        check_vma=False,
    )
```

```python
import functools
import math

import jax
import jax.numpy as jnp
from jax import lax
from jax.experimental import pallas as pl
from jax.experimental.pallas import tpu as pltpu
from jax.sharding import Mesh
from jax.sharding import PartitionSpec as P

F32 = jnp.float32
BF16 = jnp.bfloat16
PACK = 8
TAIL = 4
LANES = 128
VMEM = 56 * 1024 * 1024


def dot(a, b, contract):
    return lax.dot_general(a, b, ((contract[:1], contract[1:]), ((), ())), preferred_element_type=F32)


def scratch(blocks, rows, lanes):
    return pltpu.VMEM((lanes // LANES, blocks * (rows + 1), LANES), F32)


def spread_kernel(steps, blocks, part, pos_ref, *refs):
    *act_refs, w_ref, out_ref, buf = refs
    step = pl.program_id(0)
    wide, rows = w_ref.shape[2:]
    tiles = act_refs[0].shape[1] // LANES
    pitch = rows + 1

    @pl.when(step < steps)
    def _():
        at = pl.ds(pl.multiple_of(step * PACK * pitch, 8), PACK * pitch)
        for p in range(PACK):
            for n, ref in enumerate(act_refs):
                first = dot(w_ref[p, 0], ref[0, :, p * wide : (p + 1) * wide], (0, 1))
                for k in range(tiles):
                    buf.at[n * tiles + k, at, :][p * pitch : p * pitch + rows, :] = first[:, k * LANES : (k + 1) * LANES]

    @pl.when(step >= steps)
    def _():
        for p in range(TAIL):
            c = (step - steps) * TAIL + p
            for s in range(part):
                for k in range(buf.shape[0]):
                    rest = buf[k, pl.ds(c * part + s, blocks, stride=pitch), :]
                    out_ref[p, s * blocks : (s + 1) * blocks, k * LANES : (k + 1) * LANES] = rest.astype(BF16)


def spread(pos, acts, w, which, part):
    blocks, _, wide, rows = w.shape
    quarters, count, span = acts[0].shape
    lanes = count * len(acts)
    steps = blocks // PACK
    per = span // (PACK * wide)
    own_c = rows // part

    def act_map(i, pos):
        j = jnp.minimum(i, steps - 1)
        return j // per, 0, lax.rem(j, per)

    def w_map(i, pos):
        j = jnp.minimum(i, steps - 1)
        return lax.rem(j // per + 4 - pos[0], 4) * per + lax.rem(j, per), which, 0, 0

    return pl.pallas_call(
        functools.partial(spread_kernel, steps, blocks, part),
        grid_spec=pltpu.PrefetchScalarGridSpec(
            num_scalar_prefetch=1,
            grid=(steps + own_c // TAIL,),
            in_specs=[pl.BlockSpec((1, count, PACK * wide), act_map)] * len(acts) + [pl.BlockSpec((PACK, 1, wide, rows), w_map)],
            out_specs=pl.BlockSpec((TAIL, blocks * part, lanes), lambda i, pos: (jnp.maximum(i - steps, 0), 0, 0)),
            scratch_shapes=[scratch(blocks, rows, lanes)],
        ),
        out_shape=jax.ShapeDtypeStruct((own_c, blocks * part, lanes), BF16),
        compiler_params=pltpu.CompilerParams(vmem_limit_bytes=VMEM),
        cost_estimate=pl.CostEstimate(flops=2 * blocks * rows * wide * lanes, bytes_accessed=58_000_000, transcendentals=0),
        name="spread",
    )(pos, *acts, w)


def gather_kernel(lead, blocks, part, pos_ref, mixed_ref, *refs):
    *act_refs, w_ref, keep_ref, send_ref, grad_ref, buf = refs
    step = pl.program_id(0)
    wide, rows = w_ref.shape[2:]
    count = act_refs[0].shape[1]
    pitch = rows + 1

    @pl.when(step < lead)
    def _():
        for p in range(TAIL):
            c = step * TAIL + p
            for s in range(part):
                for k in range(buf.shape[0]):
                    rest = mixed_ref[p, s * blocks : (s + 1) * blocks, k * LANES : (k + 1) * LANES]
                    buf[k, pl.ds(c * part + s, blocks, stride=pitch), :] = rest.astype(F32)

    @pl.when(step >= lead)
    def _():
        quarter_steps = (blocks // PACK) // 4
        r = (step - lead) // quarter_steps
        t = lax.rem(r + pos_ref[0], 4)
        group = t * quarter_steps + lax.rem(step - lead, quarter_steps)
        at = pl.ds(pl.multiple_of(group * PACK * pitch, 8), PACK * pitch)
        outs = []
        for p in range(PACK):
            tiles = [buf.at[k, at, :][p * pitch : p * pitch + rows, :].astype(BF16) for k in range(buf.shape[0])]
            z = jnp.concatenate(tiles, axis=1)
            outs.append(dot(w_ref[p, 0], z, (1, 0)))
            g = 0.0
            for n, ref in enumerate(act_refs):
                g = g + dot(z[:, n * count : (n + 1) * count], ref[0, :, p * wide : (p + 1) * wide], (1, 0))
            top, left = divmod(p, PACK // 2)
            grad_ref[0, top, :, left * wide : (left + 1) * wide] = g.astype(BF16)
        out = jnp.concatenate(outs, axis=0).T.astype(BF16)
        for n in range(len(act_refs)):
            ref = keep_ref if n < len(act_refs) // 2 else send_ref
            ref[n % (len(act_refs) // 2), 0] = out[n * count : (n + 1) * count]


def gather(pos, mixed, acts, w, which, part):
    blocks, _, wide, rows = w.shape
    quarters, count, span = acts[0].shape
    half = len(acts) // 2
    lanes = count * len(acts)
    per = span // (PACK * wide)
    own_c = rows // part
    lead = own_c // TAIL
    steps = blocks // PACK

    def place(i, pos):
        j = jnp.maximum(i - lead, 0)
        return lax.rem(j // per + pos[0], 4), lax.rem(j, per)

    def act_map(i, pos):
        t, k = place(i, pos)
        return t, 0, k

    def out_map(i, pos):
        t, k = place(i, pos)
        return 0, t, 0, k

    def grad_map(i, pos):
        t, k = place(i, pos)
        return t * per + k, 0, 0, 0

    act = pl.BlockSpec((1, count, PACK * wide), act_map)
    out = pl.BlockSpec((half, 1, count, PACK * wide), out_map)
    return pl.pallas_call(
        functools.partial(gather_kernel, lead, blocks, part),
        grid_spec=pltpu.PrefetchScalarGridSpec(
            num_scalar_prefetch=1,
            grid=(lead + steps,),
            in_specs=[pl.BlockSpec((TAIL, blocks * part, lanes), lambda i, pos: (jnp.minimum(i, lead - 1), 0, 0))]
            + [act] * len(acts)
            + [pl.BlockSpec((PACK, 1, wide, rows), lambda i, pos: (jnp.maximum(i - lead, 0), which, 0, 0))],
            out_specs=[out, out, pl.BlockSpec((1, 2, rows, PACK // 2 * wide), grad_map)],
            scratch_shapes=[scratch(blocks, rows, lanes)],
        ),
        out_shape=[jax.ShapeDtypeStruct((half, quarters, count, span), BF16)] * 2
        + [jax.ShapeDtypeStruct((steps, 2, rows, PACK // 2 * wide), BF16)],
        compiler_params=pltpu.CompilerParams(vmem_limit_bytes=VMEM),
        cost_estimate=pl.CostEstimate(flops=4 * blocks * rows * wide * lanes, bytes_accessed=76_000_000, transcendentals=0),
        name="gather",
    )(pos, mixed, *acts, w)


K0 = math.sqrt(2.0 / math.pi)


def forward_kernel(at_ref, wat_ref, m_ref, li_ref, ro_ref, *refs):
    out_ref = refs[-1]
    pre = dot(li_ref[0, 0], m_ref[0], (0, 0))
    hidden = pre * (0.5 * (1.0 + jnp.tanh(K0 * (pre + 0.044715 * (pre * pre * pre)))))
    out_ref[0] = dot(ro_ref[0, 0], hidden.astype(BF16), (0, 0)).astype(BF16)


def forward(at, wat, mixed, w, second):
    count = at.shape[0]
    _, hid, tokens = mixed.shape
    act = pl.BlockSpec((1, hid, tokens), lambda i, at, wat: (at[i], 0, 0))
    old = [] if second is None else [second]
    return pl.pallas_call(
        forward_kernel,
        grid_spec=pltpu.PrefetchScalarGridSpec(
            num_scalar_prefetch=2,
            grid=(count,),
            in_specs=[
                act,
                pl.BlockSpec((1, 1, hid, hid), lambda i, at, wat: (wat[i], 0, 0, 0)),
                pl.BlockSpec((1, 1, hid, hid), lambda i, at, wat: (wat[i], 1, 0, 0)),
            ]
            + [pl.BlockSpec(memory_space=pl.ANY)] * len(old),
            out_specs=act,
        ),
        out_shape=jax.ShapeDtypeStruct(mixed.shape, BF16),
        input_output_aliases={5: 0} if old else {},
        compiler_params=pltpu.CompilerParams(vmem_limit_bytes=VMEM),
        cost_estimate=pl.CostEstimate(flops=4 * count * hid * hid * tokens, bytes_accessed=count * 8_000_000, transcendentals=0),
        name="forward",
    )(at, wat, mixed, w, w, *old)


def backward_kernel(blocks, at_ref, wat_ref, m_ref, b_ref, li_ref, ro_ref, b_out, grad_ref, bp):
    m = m_ref[0]
    li = li_ref[0, 0]
    pre = dot(li, m, (0, 0))
    square = pre * pre
    th = jnp.tanh(K0 * (pre * (1.0 + 0.044715 * square)))
    cdf = 0.5 * (1.0 + th)
    hidden = (pre * cdf).astype(BF16)
    slope = cdf + pre * (0.5 * K0) * (1.0 - th * th) * (1.0 + (3.0 * 0.044715) * square)
    bp[...] = (dot(ro_ref[0, 0], b_ref[0], (1, 0)) * slope).astype(BF16)
    b_out[0] = dot(li, bp[...], (1, 0)).astype(BF16)
    g_li = dot(bp[...], m, (1, 1)).astype(BF16)
    g_ro = dot(b_ref[0], hidden, (1, 1)).astype(BF16)
    chunks, rows = grad_ref.shape[2:4]
    piece = blocks // chunks
    for q in range(chunks):
        grad_ref[0, 0, q] = g_li[q * rows : (q + 1) * rows]
        for s in range(rows // piece):
            start = s * blocks + q * piece
            grad_ref[0, 1, q, s * piece : (s + 1) * piece, :] = g_ro[start : start + piece]


def backward(at, wat, mixed, back, w, blocks):
    count = at.shape[0]
    _, hid, tokens = mixed.shape
    act = pl.BlockSpec((1, hid, tokens), lambda i, at, wat: (at[i], 0, 0))
    return pl.pallas_call(
        functools.partial(backward_kernel, blocks),
        grid_spec=pltpu.PrefetchScalarGridSpec(
            num_scalar_prefetch=2,
            grid=(count,),
            in_specs=[
                act,
                act,
                pl.BlockSpec((1, 1, hid, hid), lambda i, at, wat: (wat[i], 0, 0, 0)),
                pl.BlockSpec((1, 1, hid, hid), lambda i, at, wat: (wat[i], 1, 0, 0)),
            ],
            out_specs=[act, pl.BlockSpec((1, 2, 4, hid // 4, hid), lambda i, at, wat: (i, 0, 0, 0, 0))],
            scratch_shapes=[pltpu.VMEM((hid, tokens), BF16)],
        ),
        out_shape=[jax.ShapeDtypeStruct(mixed.shape, BF16), jax.ShapeDtypeStruct((count, 2, 4, hid // 4, hid), BF16)],
        input_output_aliases={3: 0},
        compiler_params=pltpu.CompilerParams(vmem_limit_bytes=VMEM),
        cost_estimate=pl.CostEstimate(flops=10 * count * hid * hid * tokens, bytes_accessed=count * 15_000_000, transcendentals=0),
        name="backward",
    )(at, wat, mixed, back, w, w)


def swap(a, axis):
    return lax.ppermute(a, axis, [(0, 1), (1, 0)])


def after(value, *others):
    return lax.optimization_barrier((value, *others))[0]


def up(a, first, last):
    return lax.ppermute(a, "tensor", [(i, i + 1) for i in range(first, last)])


def down(a, first, last):
    return lax.ppermute(a, "tensor", [(i, i - 1) for i in range(first, last, -1)])


def add(*terms):
    total = terms[0].astype(F32)
    for term in terms[1:]:
        total = total + term.astype(F32)
    return total


def all_to_all(a):
    return lax.all_to_all(a, "tensor", split_axis=0, concat_axis=0, tiled=True)


def tokens_plan(tokens, cotangent, right_in, left_in, right_out, left_out):
    g = lax.axis_index("groups")
    z = lax.axis_index("tensor")
    x = lax.axis_index("x")
    core = lax.axis_index("core")
    mate = 2 * x + core
    rows, span = tokens.shape
    nb, wide, hid = right_in.shape
    blocks = 4 * nb
    part = hid // blocks
    own_nb = nb // 4
    scale = 1.0 / math.sqrt(rows * 4)
    pos = jnp.stack([z, x]).astype(jnp.int32)

    place = jnp.arange(hid)
    reorder = (place[:, None] % blocks * part + place[:, None] // blocks == place[None, :]).astype(BF16)

    def selected(u1, d1, u2, d2, u3, d3):
        return jnp.stack([jnp.where(z == 3, u3, d1), jnp.where(z < 2, d2, u2), jnp.where(z == 0, d3, u1)])

    def line_gather(a):
        u1, d1 = up(a, 0, 3), down(a, 3, 0)
        u2, d2 = up(u1, 1, 3), down(d1, 2, 0)
        return u1, d1, u2, d2, up(u2, 2, 3), down(d2, 1, 0)

    def by_group(a, b):
        return jnp.where(g == 0, jnp.stack([a, b], axis=1), jnp.stack([b, a], axis=1))

    small = jnp.stack([right_in, jnp.swapaxes(left_out, 1, 2)], axis=1)
    small = small.reshape(nb, 2, wide, 4, 4, own_nb * part)
    small = lax.dynamic_index_in_dim(small, mate, axis=4, keepdims=False).reshape(nb, 2, wide, hid // 4)
    fs = selected(*line_gather(lax.dynamic_slice_in_dim(small, g * (nb // 2), nb // 2, axis=0)))

    own_li = lax.dynamic_slice_in_dim(left_in, mate * own_nb, own_nb, axis=0)
    own_ro = lax.dynamic_slice_in_dim(right_out, mate * own_nb, own_nb, axis=0)
    own_li = jnp.einsum("pk,ckm->cpm", reorder, own_li, preferred_element_type=F32).astype(BF16)
    own_ro = jnp.einsum("cmn,pn->cmp", own_ro, reorder, preferred_element_type=F32).astype(BF16)
    own_w = jnp.stack([own_li, own_ro], axis=1)

    own_x = all_to_all(tokens.reshape(4, rows // 4, span))
    x_x = swap(own_x, "x")
    cotangent, own_x, fs, own_w = lax.optimization_barrier((cotangent, own_x, fs, own_w))
    own_y = all_to_all(cotangent.reshape(4, rows // 4, span))
    acts_x = [own_x, x_x, swap(own_x, "core"), swap(x_x, "core")]
    mine = lax.dynamic_slice_in_dim(own_w, 2 * g, 2, axis=0)
    u1, d1 = up(mine, 0, 3), down(mine, 3, 0)
    own_y, ys, u1, d1 = lax.optimization_barrier((own_y, swap(fs, "groups"), u1, d1))
    u2, d2 = up(u1, 1, 3), down(d1, 2, 0)
    small = jnp.concatenate([small, by_group(fs, ys).reshape(3 * nb, *small.shape[1:])])
    mixed = spread(pos, acts_x, small, 0, part)
    x_y = swap(own_y, "x")
    u2, d2, mixed = lax.optimization_barrier((u2, d2, mixed))
    hops = u1, d1, u2, d2, up(u2, 2, 3), down(d2, 1, 0)
    order = [(gr, h) for gr in range(2) for h in range(2)]
    index = {(gr, h): 2 * ((g + gr) % 2) + h for gr, h in order}
    six = jnp.arange(6, dtype=jnp.int32)
    own_at = jnp.stack([z * own_nb + index[o] for o in order]).astype(jnp.int32)
    own_wat = jnp.stack([index[o] for o in order]).astype(jnp.int32)
    second = forward(own_at, own_wat, mixed, own_w, None)
    x_y, second, *hops = lax.optimization_barrier((x_y, second, *hops))
    acts_y = [own_y, x_y, swap(own_y, "core"), swap(x_y, "core")]
    f, x_y = lax.optimization_barrier((selected(*hops), x_y))
    yf = swap(f, "groups")
    back = spread(pos, acts_y, small, 1, part)
    pieces = [(own_at, own_wat, own_w)]
    for gr, w in enumerate((f, yf)):
        at = [(z + r) % 4 * own_nb + index[gr, h] for r in (1, 2, 3) for h in range(2)]
        pieces.append((jnp.stack(at).astype(jnp.int32), six, w.reshape(6, 2, hid, hid)))

    def step(n):
        at, wat, w = pieces[n]
        return backward(at, wat, mixed, back, w, blocks)

    def step_forward(n):
        at, wat, w = pieces[n]
        return forward(at, wat, mixed, w, second)

    def line(n):
        return grads[n].reshape(3, -1, hid // 4, hid)

    def plus(a, u, d):
        return add(a, u).astype(BF16), add(a, d).astype(BF16)

    def plus_two(a, u, b, d):
        return add(a, u).astype(BF16), add(b, d).astype(BF16)

    hold = lax.optimization_barrier
    grads = {}
    back, grads[1] = step(1)
    s1 = line(1)
    u, d = up(s1[2], 0, 1), down(s1[0], 3, 2)
    back, second = hold((back, second))
    second = step_forward(1)
    back, second = hold((back, second))
    back, grads[0] = step(0)
    back, u, d = hold((back, u, d))
    back, u, d = hold((back, *plus(s1[1], u, d)))
    u, d = up(u, 0, 2), down(d, 3, 1)
    back, grads[2] = step(2)
    s2 = line(2)
    v, e = up(s2[2], 0, 1), down(s2[0], 3, 2)
    back, u, d = hold((back, u, d))
    back, u, d = hold((back, *plus_two(s1[0], u, s1[2], d)))
    u1, d1 = up(u, 0, 3), down(d, 3, 0)
    keep, send, ri = gather(pos, back, acts_x, small, 0, part)
    second, keep, send, v, e = hold((second, keep, send, v, e))
    got = swap(send, "core")
    ri = lax.psum_scatter(ri.reshape(4, -1, hid // 4, hid), "tensor", scatter_dimension=0)
    second, v, e = hold((second, *plus(s2[1], v, e)))
    v, e = up(v, 0, 2), down(e, 3, 1)
    second = step_forward(2)
    second, got, u1, d1 = hold((second, got, u1, d1))
    second, gx_x = hold((second, add(keep[1], got[1]).astype(BF16)))
    gx_x = swap(gx_x, "x")
    gx = add(keep[0], got[0])
    keep, send, lo = gather(pos, second, acts_y, small, 1, part)
    send, v, e = hold((send, v, e))
    v, e = plus_two(s2[0], v, s2[2], e)
    v1, e1 = up(v, 0, 3), down(e, 3, 0)
    gx_x, send, v1, e1, ri = hold((gx_x, send, v1, e1, ri))
    gx = add(gx, gx_x).astype(BF16)
    grad_tokens = all_to_all(gx).reshape(rows, span)
    got = swap(send, "core")
    lo = lax.psum_scatter(lo.reshape(4, -1, hid // 4, hid), "tensor", scatter_dimension=0)
    out_x = swap(add(keep[1], got[1]).astype(BF16), "x")
    output = all_to_all(add(add(keep[0], got[0]), out_x).astype(BF16)).reshape(rows, span)

    def split(total):
        total = total.reshape(-1, 2, 2, total.shape[1] // 4, hid).transpose(1, 2, 0, 3, 4).reshape(2, 2, -1, hid)
        kept = lax.dynamic_index_in_dim(total, x, axis=0, keepdims=False)
        got = swap(lax.dynamic_index_in_dim(total, 1 - x, axis=0, keepdims=False), "x")
        total = jnp.where(x == 0, jnp.stack([kept, got], axis=1), jnp.stack([got, kept], axis=1))
        kept = lax.dynamic_index_in_dim(total, core, axis=0, keepdims=False)
        got = swap(lax.dynamic_index_in_dim(total, 1 - core, axis=0, keepdims=False), "core")
        return jnp.where(core == 0, jnp.stack([kept, got], axis=1), jnp.stack([got, kept], axis=1)).reshape(4, -1, hid)

    own = grads[0].reshape(2, -1, hid // 4, hid)
    big0 = split(add(own[0], u1, d1).astype(BF16).reshape(-1, hid, hid)).reshape(4, 2, 2, hid // 4, hid)
    big1 = split(add(own[1], v1, e1).astype(BF16).reshape(-1, hid, hid)).reshape(4, 2, 2, hid // 4, hid)
    first = split(jnp.concatenate([lo, ri])).reshape(4, 2, nb // PACK, 2, hid // 16, PACK // 2, wide)
    grad_lo, grad_ri = first[:, 0], first[:, 1]
    big = by_group(big0, big1).reshape(nb, 2, hid // 4, hid)
    grad_li = jnp.einsum("cmp,pk->cmk", big[:, 0], reorder, preferred_element_type=F32) * scale
    grad_li = jnp.swapaxes(grad_li, 1, 2)
    grad_ro = big[:, 1].reshape(nb, part, blocks // 4, hid).swapaxes(1, 2).reshape(nb, hid // 4, hid).astype(F32) * scale
    grad_ro = jnp.swapaxes(grad_ro, 1, 2)
    grad_lo = grad_lo.astype(F32).transpose(1, 2, 4, 0, 3, 5).reshape(nb, hid // 4, wide) * scale
    grad_ri = grad_ri.astype(F32).transpose(1, 2, 4, 5, 0, 3).reshape(nb, wide, hid // 4) * scale
    return (output, grad_tokens, grad_ri, grad_li, grad_ro, grad_lo)


def gelu_back(pre, upstream):
    return jax.vjp(jax.nn.gelu, pre)[1](upstream)[0]


def blocks_plan(tokens, cotangent, right_in, left_in, right_out, left_out):
    f32 = jnp.float32
    bf16 = jnp.bfloat16
    rows = tokens.shape[0]
    local_blocks = right_in.shape[0]
    block_in = right_in.shape[1]
    block_hid = right_in.shape[2]
    all_blocks = local_blocks * lax.axis_size("tensor")
    part_hid = block_hid // all_blocks
    scale = 1.0 / math.sqrt(rows * lax.axis_size("dp"))
    blocks = tokens.reshape(rows, local_blocks, block_in)
    back = cotangent.reshape(rows, local_blocks, block_in)
    ri_split = right_in.reshape(local_blocks, block_in, all_blocks, part_hid)
    first = jnp.einsum("tbi,bics->cbst", blocks, ri_split, preferred_element_type=f32)
    first = first.astype(bf16).reshape(all_blocks, local_blocks * part_hid, rows)
    ro_split = right_out.reshape(local_blocks, block_hid, all_blocks, part_hid)
    arrived_first = lax.all_to_all(first, "tensor", split_axis=0, concat_axis=1, tiled=True)
    count = arrived_first.shape[2]
    pre_act = jnp.einsum("ckt,ckm->cmt", arrived_first, left_in, preferred_element_type=f32)
    hidden_act = jax.nn.gelu(pre_act).astype(bf16)
    second_act = jnp.einsum("cmt,cmds->dcst", hidden_act, ro_split, preferred_element_type=f32)
    second_act = second_act.astype(bf16).reshape(all_blocks, local_blocks * part_hid, count)
    mixed_out = lax.all_to_all(second_act, "tensor", split_axis=0, concat_axis=1, tiled=True)
    output = jnp.einsum("dkt,dkn->tdn", mixed_out, left_out, preferred_element_type=f32)
    output = output.astype(bf16).reshape(rows, local_blocks * block_in)
    grad_lo = jnp.einsum("dkt,tdn->dkn", mixed_out, back, preferred_element_type=f32) * scale
    lo_split = left_out.reshape(local_blocks, all_blocks, part_hid, block_in)
    back_mixed = jnp.einsum("tdn,dcsn->cdst", back, lo_split, preferred_element_type=f32)
    back_mixed = back_mixed.astype(bf16).reshape(all_blocks, local_blocks * part_hid, rows)
    back_second = lax.all_to_all(back_mixed, "tensor", split_axis=0, concat_axis=1, tiled=True)
    grad_ro = (
        jnp.einsum("cmt,cnt->cmn", hidden_act, back_second, preferred_element_type=f32) * scale
    )
    back_hidden = jnp.einsum("cnt,cmn->cmt", back_second, right_out, preferred_element_type=f32)
    back_pre = gelu_back(pre_act, back_hidden).astype(bf16)
    grad_li = (
        jnp.einsum("ckt,cmt->ckm", arrived_first, back_pre, preferred_element_type=f32) * scale
    )
    li_split = left_in.reshape(local_blocks, all_blocks, part_hid, block_hid)
    back_in = jnp.einsum("cmt,cbsm->bcst", back_pre, li_split, preferred_element_type=f32)
    back_in = back_in.astype(bf16).reshape(all_blocks, local_blocks * part_hid, rows)
    back_first = lax.all_to_all(back_in, "tensor", split_axis=0, concat_axis=1, tiled=True)
    grad_x = jnp.einsum("bjt,bij->tbi", back_first, right_in, preferred_element_type=f32)
    grad_tokens = grad_x.astype(bf16).reshape(rows, local_blocks * block_in)
    grad_ri = jnp.einsum("tbi,bjt->bij", blocks, back_first, preferred_element_type=f32) * scale
    grad_ri, grad_li, grad_ro, grad_lo = (
        lax.psum_scatter(grad_ri, "dp", scatter_dimension=2, tiled=True),
        lax.psum_scatter(grad_li, "dp", scatter_dimension=2, tiled=True),
        lax.psum_scatter(grad_ro, "dp", scatter_dimension=2, tiled=True),
        lax.psum_scatter(grad_lo, "dp", scatter_dimension=1, tiled=True),
    )
    return (output, grad_tokens, grad_ri, grad_li, grad_ro, grad_lo)


def solution(mesh):
    wide = mesh.shape["tensor"] == 4 and mesh.shape["dp"] == 4 and mesh.shape["groups"] == 2
    dp = "dp"
    if wide:
        dp = ("x", "core")
        mesh = Mesh(mesh.devices.reshape(2, 4, 2, 2), ("groups", "tensor", *dp))
    row = ("groups", "x", "core") if wide else ("groups", "dp")
    acts = P(row, "tensor")
    placed = (acts, acts, P("tensor", None, None), P("tensor", None, None), P("tensor", None, None), P("tensor", None, None))
    own = ("groups", "tensor")
    return jax.shard_map(
        tokens_plan if wide else blocks_plan,
        mesh=mesh,
        in_specs=placed,
        out_specs=(acts, acts, P(own, None, dp), P(own, None, dp), P(own, None, dp), P(own, dp, None)),
        check_vma=False,
    )
```
